32 devices in a mesh: tm: 16 (over z, y, x), slab: 2 (over core).
Axes of the slice: x: 2, y: 2, z: 4, core: 2. Of those that a mesh axis runs over, the one named last changes fastest.
Arguments:
- c_values: float32 [64, 8, 64, 128], P('tm', 'slab'), may hold values from -2 to 2
- initial: float32 [8, 64, 128], P('slab'), may hold values from -6 to 6
- diffusivity: float32 [8, 64, 128], P('slab'), may hold values from 0.03 to 0.12
- velocity: float32 [3, 8, 64, 128], P(None, 'slab'), may hold values from -0.09 to 0.09
- gains: float32 [64, 8, 64, 128], P('tm', 'slab'), may hold values from 0 to 1, as said below
Outputs:
- corrected: float32 [64, 8, 64, 128], P('tm', 'slab')
The draws below stay inside these ranges and needn't reach their ends.
Inputs may be any that keep to these rules, and one draw needn't show every extreme that they name: `gains`: each cell's factor over one coarse interval.
All inputs are finite; a program needn't handle non-finite values.
Results may differ from the reference program's by a relative error of at most 0.00002.
Values sent between devices are 32-bit elements; how exact they have to be, the bound alone decides.
A program may use at most 64 MiB of HBM per device.

```python
import math
import jax
import jax.numpy as jnp
from jax import lax

NX = 64
NY = 128
STEPS = 8
COARSE_POINTS = 64
NZ = 8


def draw_gains(key, part):
    key = jax.random.fold_in(key, 11)
    keys = jax.random.split(key, 6)
    slow_share = 0.5
    cell_shape = (1, NZ, NX, NY)
    picked = jax.random.uniform(keys[0], cell_shape, jnp.float32)
    slow_rate = math.log(10.0) / COARSE_POINTS * jax.random.uniform(keys[1], cell_shape, jnp.float32, 0.05, 0.35)
    fast_rate = jax.random.uniform(keys[2], cell_shape, jnp.float32, 0.36, 1.6)
    nominal_rate = jnp.where(picked < slow_share, slow_rate, fast_rate)
    random_wobble = jax.random.uniform(keys[3], (COARSE_POINTS, NZ, NX, NY), jnp.float32, 0.5, 1.5)
    location_list = jax.random.randint(keys[4], (2,), 0, COARSE_POINTS)
    forcing_magnitude = jax.random.uniform(keys[5], (2,), jnp.float32, 0.2, 0.5)
    local_step_count = jnp.arange(COARSE_POINTS)
    sudden_spike = jnp.where(local_step_count == location_list[0], 1.0 - forcing_magnitude[0], 1.0)
    sudden_spike = sudden_spike * jnp.where(local_step_count == location_list[1], 1.0 - forcing_magnitude[1], 1.0)
    return jnp.exp(-nominal_rate * random_wobble) * sudden_spike[:, None, None, None]


def level_of(rng, shape, shards, smallest, largest):
    loudness = 1.0
    for axis_at, blocks in shards:
        heights = jax.random.uniform(jax.random.fold_in(jax.random.fold_in(rng, 6), axis_at), (blocks,), jnp.float32, smallest / len(shards), largest / len(shards))
        loudness = loudness * jnp.repeat(jnp.exp(heights), shape[axis_at] // blocks).reshape((-1,) + (1,) * (len(shape) - 1 - axis_at))
    return loudness


def centred(key, shape, scale, reach, shards=(), dtype=jnp.bfloat16):
    result = scale * jax.random.normal(key, shape, jnp.float32)
    if shards:
        result = result * level_of(key, shape, shards, -0.22, 0.18)
    return jnp.clip(result, -reach, reach).astype(dtype)


def setup_inputs(seed: int = 0) -> dict:
    splits = jax.random.split(jax.random.key(seed), 6)
    c_values = centred(splits[0], (COARSE_POINTS, NZ, NX, NY), 0.25, 2.0, ((0, 16), (1, 2)), jnp.float32)
    initial = centred(splits[1], (NZ, NX, NY), 1.0, 6.0, ((0, 2),), jnp.float32)
    diffusivity = jnp.clip(jnp.exp(math.log(0.12) - 1.3862944 * jax.random.uniform(splits[2], (NZ, NX, NY), jnp.float32) ** level_of(splits[2], (NZ, NX, NY), ((0, 2),), -0.2, 0.2)), 0.03, 0.12)
    velocity = jnp.clip(jax.random.uniform(splits[3], (3, NZ, NX, NY), jnp.float32, -0.09, 0.09) * level_of(splits[3], (3, NZ, NX, NY), ((1, 2),), -0.4, 0.0), -0.09, 0.09)
    gains = draw_gains(jax.random.fold_in(splits[5], 71), 0)
    return {"c_values": c_values, "initial": initial, "diffusivity": diffusivity, "velocity": velocity, "gains": gains}


def upwind(speed, center, minus, plus):
    return jnp.maximum(speed, 0.0) * (center - minus) + jnp.minimum(speed, 0.0) * (plus - center)


def advance(field, diffusivity, velocity):
    padded = jnp.pad(field, 1)
    lower_z = padded[:-2, 1:-1, 1:-1]
    upper_z = padded[2:, 1:-1, 1:-1]
    lower_x = padded[1:-1, :-2, 1:-1]
    upper_x = padded[1:-1, 2:, 1:-1]
    lower_y = padded[1:-1, 1:-1, :-2]
    upper_y = padded[1:-1, 1:-1, 2:]
    laplace = lower_z + upper_z + lower_x + upper_x + lower_y + upper_y - 6.0 * field
    transport = upwind(velocity[0], field, lower_z, upper_z) + upwind(velocity[1], field, lower_x, upper_x) + upwind(velocity[2], field, lower_y, upper_y)
    return field + diffusivity * laplace - transport


def reference(c_values, initial, diffusivity, velocity, gains):
    def interval(carry, pieces):
        previous, error = carry
        current, factor = pieces
        moved = lax.fori_loop(0, STEPS, lambda i, v: advance(v, diffusivity, velocity), previous)
        residual = moved - current
        error = factor * error + residual
        return (current, error), current + error

    start = (initial, jnp.zeros_like(initial))
    final, corrected = lax.scan(interval, start, (c_values, gains))
    return corrected
```

```python
import functools

import jax
import jax.numpy as jnp
from jax import lax
from jax.experimental import pallas as pl
from jax.experimental.pallas import tpu as pltpu
from jax.sharding import PartitionSpec as P

STEPS = 8
MESH = pl.DeviceIdType.MESH


def padded_2(block, sides, width):
    for axis, dim in sides:
        count = lax.axis_size(axis)
        forward = [(i, i + 1) for i in range(count - 1)]
        backward = [(target, source) for source, target in forward]
        low = lax.ppermute(
            lax.slice_in_dim(block, block.shape[dim] - width, None, axis=dim), axis, forward
        )
        high = lax.ppermute(lax.slice_in_dim(block, 0, width, axis=dim), axis, backward)
        block = jnp.concatenate([low, block, high], axis=dim)
    return block


def shifted(value, axis, steps):
    count = lax.axis_size(axis)
    first, last = (max(0, -steps), min(count, count - steps))
    return lax.ppermute(value, axis, [(source, source + steps) for source in range(first, last)])


def entering_2(part, axis, combine, identity):
    place = lax.axis_index(axis)
    gathered = jax.tree.map(lambda a: lax.all_gather(a, axis), part)
    state = jax.tree.map(lambda a, e: jnp.zeros_like(a) + jnp.asarray(e, a.dtype), part, identity)

    def one(step, state):
        return combine(
            state, jax.tree.map(lambda a: lax.dynamic_index_in_dim(a, step, 0, False), gathered)
        )

    return lax.fori_loop(0, place, one, state)


def upwind(speed, center, minus, plus):
    return jnp.maximum(speed, 0.0) * (center - minus) + jnp.minimum(speed, 0.0) * (plus - center)


def advance(padded, diffusivity, velocity):
    center = padded[:, 1:-1]
    lower_z = padded[:, :-2]
    upper_z = padded[:, 2:]
    flat = jnp.pad(center, ((0, 0), (0, 0), (1, 1), (1, 1)))
    lower_x = flat[:, :, :-2, 1:-1]
    upper_x = flat[:, :, 2:, 1:-1]
    lower_y = flat[:, :, 1:-1, :-2]
    upper_y = flat[:, :, 1:-1, 2:]
    laplace = lower_z + upper_z + lower_x + upper_x + lower_y + upper_y - 6.0 * center
    transport = (
        upwind(velocity[0], center, lower_z, upper_z)
        + upwind(velocity[1], center, lower_x, upper_x)
        + upwind(velocity[2], center, lower_y, upper_y)
    )
    return center + diffusivity * laplace - transport


def propagate(field, diffusivity, velocity):
    for step in range(STEPS):
        padded = padded_2(field, (("slab", 1),), 1)
        field = advance(padded, diffusivity, velocity)
    return field


def combine_maps(earlier, later):
    return (earlier[0] * later[0], later[0] * earlier[1] + later[1])


def body(c_values, initial, diffusivity, velocity, gains):
    count = c_values.shape[0]
    is_first = lax.axis_index("tm") == 0
    received = shifted(c_values[-1], "tm", 1)
    previous = jnp.where(is_first, initial, received)
    starts = jnp.concatenate([previous[None], c_values[:-1]], 0)
    ends = propagate(starts, diffusivity, velocity)
    residual = ends - c_values
    error = jnp.zeros_like(initial)
    product = jnp.ones_like(initial)
    for index_k in range(count):
        error = gains[index_k] * error + residual[index_k]
        product = product * gains[index_k]
    identity = (jnp.ones_like(initial), jnp.zeros_like(initial))
    entering = entering_2((product, error), "tm", combine_maps, identity)
    error = entering[1]
    results = []
    for index_k in range(count):
        error = gains[index_k] * error + residual[index_k]
        results.append(c_values[index_k] + error)
    return jnp.stack(results, 0)


def fused_kernel(
    n, nx, half,
    c_hbm, init_hbm, diff_hbm, vel_hbm, gains_hbm, out_ref,
    c_own, g_own, raw, coef, first, second, spare, ends,
    base, cum, block_e, all_p, all_e, leave, enter,
    local_sem, swap_send, swap_recv, start_send, start_recv, ends_send, ends_recv,
    p_send, p_recv, e_send, e_recv, x_send, x_recv,
):
    t, s = lax.axis_index("tm"), lax.axis_index("slab")
    other = 1 - s
    lanes = c_own.shape[-1]
    planes = half // nx
    whole = 2 * half
    part = half // n
    mine = pl.ds(pl.multiple_of(s * half, half), half)
    theirs = pl.ds(pl.multiple_of(other * half, half), half)
    mine_in = pl.ds(pl.multiple_of(nx + s * half, nx), half)
    theirs_in = pl.ds(pl.multiple_of(nx + other * half, nx), half)

    barrier = pltpu.get_barrier_semaphore()

    def greet(where):
        pl.semaphore_signal(barrier, inc=1, device_id=where, device_id_type=MESH)

    def hello(d, carry):
        greet((lax.rem(t + d, n), s))
        return carry

    zero = jnp.zeros((nx, lanes), jnp.float32)
    for field in (first, second, spare):
        field[0:nx] = zero
        field[nx + whole : 2 * nx + whole] = zero

    greet((t, other))

    @pl.when((s == 0) & (t > 0))
    def _():
        greet((t - 1, other))

    @pl.when((s == 1) & (t < n - 1))
    def _():
        greet((t + 1, other))

    lax.fori_loop(1, n, hello, 0)

    local_diff = pltpu.make_async_copy(diff_hbm, raw.at[0, mine], local_sem.at[0])
    local_vel = pltpu.make_async_copy(vel_hbm, raw.at[1:4, mine], local_sem.at[1])
    local_c = pltpu.make_async_copy(c_hbm, c_own, local_sem.at[2])
    local_g = pltpu.make_async_copy(gains_hbm, g_own, local_sem.at[3])
    local_first = pltpu.make_async_copy(c_hbm.at[2 * s], first.at[mine_in], local_sem.at[4])
    local_second = pltpu.make_async_copy(c_hbm.at[1], second.at[mine_in], local_sem.at[5])
    local_init = pltpu.make_async_copy(init_hbm, second.at[mine_in], local_sem.at[6])
    local_diff.start()
    local_vel.start()
    local_first.start()

    @pl.when(s == 1)
    def _():
        local_second.start()

    @pl.when((s == 0) & (t == 0))
    def _():
        local_init.start()

    local_g.start()
    local_c.start()

    extra = jnp.where(s == 0, jnp.where(t > 0, 1, 0), jnp.where(t < n - 1, 1, 0))
    pl.semaphore_wait(barrier, n + extra)

    def remote(src, dst, send, recv, where):
        return pltpu.make_async_remote_copy(
            src_ref=src, dst_ref=dst, send_sem=send, recv_sem=recv,
            device_id=where, device_id_type=MESH,
        )

    swap_first = remote(
        c_hbm.at[2 * other], first.at[mine_in], swap_send.at[0], swap_recv.at[0], (t, other)
    )
    swap_diff = remote(diff_hbm, raw.at[0, mine], swap_send.at[1], swap_recv.at[1], (t, other))
    swap_vel = remote(vel_hbm, raw.at[1:4, mine], swap_send.at[2], swap_recv.at[2], (t, other))
    to_next = remote(
        c_hbm.at[3], second.at[mine_in], start_send.at[0], start_recv.at[s], (t + 1, 0)
    )
    to_upper = remote(
        c_hbm.at[1], second.at[mine_in], start_send.at[1], start_recv.at[s], (t, 1)
    )
    to_lower = remote(
        init_hbm, second.at[mine_in], start_send.at[2], start_recv.at[s], (t, 0)
    )

    @pl.when(t < n - 1)
    def _():
        to_next.start()

    swap_diff.start()
    swap_vel.start()
    swap_first.start()

    @pl.when(s == 0)
    def _():
        to_upper.start()

    @pl.when((s == 1) & (t == 0))
    def _():
        to_lower.start()

    row = lax.broadcasted_iota(jnp.int32, (nx, lanes), 0)
    lane = lax.broadcasted_iota(jnp.int32, (nx, lanes), 1)

    def coefficients(start):
        def plane(z, carry):
            at = pl.ds(pl.multiple_of(start + z * nx, nx), nx)
            d = raw[0, at]
            centre = 1.0 - 6.0 * d
            for q in range(3):
                speed = raw[q + 1, at]
                up = jnp.maximum(speed, 0.0)
                down = jnp.minimum(speed, 0.0)
                centre = centre - up + down
                minus = d + up
                plus = d - down
                if q == 1:
                    minus = jnp.where(row == 0, 0.0, minus)
                    plus = jnp.where(row == nx - 1, 0.0, plus)
                if q == 2:
                    minus = jnp.where(lane == 0, 0.0, minus)
                    plus = jnp.where(lane == lanes - 1, 0.0, plus)
                coef[1 + 2 * q, at] = minus
                coef[2 + 2 * q, at] = plus
            coef[0, at] = centre
            return carry

        lax.fori_loop(0, planes, plane, 0)

    local_diff.wait()
    local_vel.wait()
    coefficients(s * half)

    local_g.wait()

    def products(z, carry):
        at = pl.ds(pl.multiple_of(z * nx, nx), nx)
        p = g_own[0, at]
        cum[0, at] = p
        for k in range(1, 4):
            p = p * g_own[k, at]
            cum[k, at] = p
        return carry

    lax.fori_loop(0, planes, products, 0)

    def share(q):
        return pl.ds(pl.multiple_of(q * part, part), part)

    def p_copy(peer, index):
        return remote(
            cum.at[3, share(peer)], all_p.at[t], p_send.at[index], p_recv.at[t], (peer, s)
        )

    def e_copy(peer, index):
        return remote(
            block_e.at[share(peer)], all_e.at[t], e_send.at[index], e_recv.at[t], (peer, s)
        )

    def x_copy(peer, index):
        return remote(
            leave.at[peer], enter.at[share(t)], x_send.at[index], x_recv.at[t], (peer, s)
        )

    def send_all(copy):
        def one(d, carry):
            copy(lax.rem(t + d, n), d).start()
            return carry

        lax.fori_loop(1, n, one, 0)

    swap_diff.wait_recv()
    swap_vel.wait_recv()
    coefficients(other * half)

    def step(src, dst):
        for z in range(2 * planes):
            at = nx + z * nx
            here = z * nx
            v = src[at : at + nx]
            new = coef[0, here : here + nx] * v
            new += coef[1, here : here + nx] * src[at - nx : at]
            new += coef[2, here : here + nx] * src[at + nx : at + 2 * nx]
            new += coef[3, here : here + nx] * src[at - 1 : at + nx - 1]
            new += coef[4, here : here + nx] * src[at + 1 : at + nx + 1]
            new += coef[5, here : here + nx] * pltpu.roll(v, 1, 1)
            new += coef[6, here : here + nx] * pltpu.roll(v, lanes - 1, 1)
            dst[at : at + nx] = new

    def propagated(field):
        def pair(i, carry):
            step(field, spare)
            step(spare, field)
            return carry

        lax.fori_loop(0, STEPS // 2, pair, 0)

    local_first.wait()
    swap_first.wait_recv()
    send_all(p_copy)
    propagated(first)

    back_first = remote(
        first.at[theirs_in], ends.at[1], ends_send.at[0], ends_recv.at[0], (t, other)
    )
    back_first.start()

    @pl.when(s == 1)
    def _():
        local_second.wait()

    @pl.when((s == 0) & (t == 0))
    def _():
        local_init.wait()

    @pl.when((s == 1) | (t > 0))
    def _():
        remote(
            c_hbm.at[3], second.at[nx : nx + half], start_send.at[0], start_recv.at[0], (t, other)
        ).wait_recv()

    @pl.when(s == 0)
    def _():
        remote(
            c_hbm.at[3], second.at[nx + half : nx + whole],
            start_send.at[0], start_recv.at[1], (t, other),
        ).wait_recv()

    propagated(second)
    back_second = remote(
        second.at[theirs_in], ends.at[0], ends_send.at[1], ends_recv.at[1], (t, other)
    )
    back_second.start()
    local_c.wait()
    back_first.wait_recv()
    back_second.wait_recv()

    def local_errors(lower):
        def plane(z, carry):
            at = pl.ds(pl.multiple_of(z * nx, nx), nx)
            own_at = pl.ds(pl.multiple_of(nx + s * half + z * nx, nx), nx)
            own = [second[own_at], first[own_at]]
            got = [ends[0, at], ends[1, at]]
            finals = own + got if lower else got + own
            error = jnp.zeros((nx, lanes), jnp.float32)
            for k in range(4):
                c = c_own[k, at]
                error = g_own[k, at] * error + (finals[k] - c)
                base[k, at] = error + c
            block_e[at] = error
            return carry

        lax.fori_loop(0, planes, plane, 0)

    @pl.when(s == 0)
    def _():
        local_errors(True)

    @pl.when(s == 1)
    def _():
        local_errors(False)

    send_all(e_copy)
    all_p[t] = cum[3, share(t)]
    all_e[t] = block_e[share(t)]

    def scan(i, state):
        @pl.when(i != t)
        def _():
            remote(
                cum.at[3, share(i)], all_p.at[i], p_send.at[0], p_recv.at[i], (i, s)
            ).wait_recv()
            remote(
                block_e.at[share(i)], all_e.at[i], e_send.at[0], e_recv.at[i], (i, s)
            ).wait_recv()

        leave[i] = state

        @pl.when(i != t)
        def _():
            x_copy(i, i).start()

        return all_p[i] * state + all_e[i]

    lax.fori_loop(0, n, scan, jnp.zeros((part, lanes), jnp.float32))
    enter[share(t)] = leave[t]

    def finish(q, carry):
        @pl.when(q != t)
        def _():
            remote(
                leave.at[q], enter.at[share(q)], x_send.at[q], x_recv.at[q], (q, s)
            ).wait_recv()

        at = share(q)
        entering = enter[at]
        for k in range(4):
            out_ref[k, at] = base[k, at] + cum[k, at] * entering
        return carry

    lax.fori_loop(0, n, finish, 0)

    swap_first.wait_send()
    swap_diff.wait_send()
    swap_vel.wait_send()

    @pl.when(t < n - 1)
    def _():
        to_next.wait_send()

    @pl.when(s == 0)
    def _():
        to_upper.wait_send()

    @pl.when((s == 1) & (t == 0))
    def _():
        to_lower.wait_send()

    back_first.wait_send()
    back_second.wait_send()

    def drain(d, carry):
        peer = lax.rem(t + d, n)
        p_copy(peer, d).wait_send()
        e_copy(peer, d).wait_send()
        x_copy(peer, peer).wait_send()
        return carry

    lax.fori_loop(1, n, drain, 0)


def fused(c_values, initial, diffusivity, velocity, gains):
    n = lax.axis_size("tm")
    count, nz, nx, ny = c_values.shape
    half = nz * nx
    part = half // n
    f32 = jnp.float32
    dma = pltpu.SemaphoreType.DMA
    field = pltpu.VMEM((2 * half + 2 * nx, ny), f32)
    block = pltpu.VMEM((half, ny), f32)
    four = pltpu.VMEM((4, half, ny), f32)
    shares = pltpu.VMEM((n, part, ny), f32)
    out = pl.pallas_call(
        functools.partial(fused_kernel, n, nx, half),
        out_shape=jax.ShapeDtypeStruct((count, half, ny), f32),
        in_specs=[pl.BlockSpec(memory_space=pl.ANY)] * 5,
        out_specs=pl.BlockSpec(memory_space=pltpu.VMEM),
        scratch_shapes=[
            four, four,
            pltpu.VMEM((4, 2 * half, ny), f32),
            pltpu.VMEM((7, 2 * half, ny), f32),
            field, field, field,
            pltpu.VMEM((2, half, ny), f32),
            four, four, block, shares, shares, shares, block,
            dma((7,)), dma((3,)), dma((3,)), dma((3,)), dma((2,)), dma((2,)), dma((2,)),
            dma((n,)), dma((n,)), dma((n,)), dma((n,)), dma((n,)), dma((n,)),
        ],
        compiler_params=pltpu.CompilerParams(
            collective_id=0, has_side_effects=True, vmem_limit_bytes=32 * 1024 * 1024
        ),
    )(
        c_values.reshape(count, half, ny),
        initial.reshape(half, ny),
        diffusivity.reshape(half, ny),
        velocity.reshape(3, half, ny),
        gains.reshape(count, half, ny),
    )
    return out.reshape(c_values.shape)


def planned(c_values, initial, diffusivity, velocity, gains):
    n, slabs = lax.axis_size("tm"), lax.axis_size("slab")
    count, nz, nx, ny = c_values.shape
    fits = slabs == 2 and count == 4 and n > 1 and nx % 8 == 0 and ny % 128 == 0
    if fits and (nz * nx) % (8 * n) == 0:
        return fused(c_values, initial, diffusivity, velocity, gains)
    return body(c_values, initial, diffusivity, velocity, gains)


def solution(mesh):
    placed = (
        P("tm", "slab", None, None),
        P("slab", None, None),
        P("slab", None, None),
        P(None, "slab", None, None),
        P("tm", "slab", None, None),
    )
    return jax.shard_map(
        planned, mesh=mesh, in_specs=placed, out_specs=P("tm", "slab", None, None), check_vma=False
    )
```

```python
import functools

import jax
import jax.numpy as jnp
from jax import lax
from jax.experimental import pallas as pl
from jax.experimental.pallas import tpu as pltpu
from jax.sharding import PartitionSpec as P

STEPS = 8
GROUP = 4
MESH = pl.DeviceIdType.MESH


def padded_2(block, sides, width):
    for axis, dim in sides:
        count = lax.axis_size(axis)
        forward = [(i, i + 1) for i in range(count - 1)]
        backward = [(target, source) for source, target in forward]
        low = lax.ppermute(
            lax.slice_in_dim(block, block.shape[dim] - width, None, axis=dim), axis, forward
        )
        high = lax.ppermute(lax.slice_in_dim(block, 0, width, axis=dim), axis, backward)
        block = jnp.concatenate([low, block, high], axis=dim)
    return block


def shifted(value, axis, steps):
    count = lax.axis_size(axis)
    first, last = (max(0, -steps), min(count, count - steps))
    return lax.ppermute(value, axis, [(source, source + steps) for source in range(first, last)])


def entering_2(part, axis, combine, identity):
    place = lax.axis_index(axis)
    gathered = jax.tree.map(lambda a: lax.all_gather(a, axis), part)
    state = jax.tree.map(lambda a, e: jnp.zeros_like(a) + jnp.asarray(e, a.dtype), part, identity)

    def one(step, state):
        return combine(
            state, jax.tree.map(lambda a: lax.dynamic_index_in_dim(a, step, 0, False), gathered)
        )

    return lax.fori_loop(0, place, one, state)


def upwind(speed, center, minus, plus):
    return jnp.maximum(speed, 0.0) * (center - minus) + jnp.minimum(speed, 0.0) * (plus - center)


def advance(padded, diffusivity, velocity):
    center = padded[:, 1:-1]
    lower_z = padded[:, :-2]
    upper_z = padded[:, 2:]
    flat = jnp.pad(center, ((0, 0), (0, 0), (1, 1), (1, 1)))
    lower_x = flat[:, :, :-2, 1:-1]
    upper_x = flat[:, :, 2:, 1:-1]
    lower_y = flat[:, :, 1:-1, :-2]
    upper_y = flat[:, :, 1:-1, 2:]
    laplace = lower_z + upper_z + lower_x + upper_x + lower_y + upper_y - 6.0 * center
    transport = (
        upwind(velocity[0], center, lower_z, upper_z)
        + upwind(velocity[1], center, lower_x, upper_x)
        + upwind(velocity[2], center, lower_y, upper_y)
    )
    return center + diffusivity * laplace - transport


def propagate(field, diffusivity, velocity):
    for step in range(STEPS):
        padded = padded_2(field, (("slab", 1),), 1)
        field = advance(padded, diffusivity, velocity)
    return field


def combine_maps(earlier, later):
    return (earlier[0] * later[0], later[0] * earlier[1] + later[1])


def body(c_values, initial, diffusivity, velocity, gains):
    count = c_values.shape[0]
    is_first = lax.axis_index("tm") == 0
    received = shifted(c_values[-1], "tm", 1)
    previous = jnp.where(is_first, initial, received)
    starts = jnp.concatenate([previous[None], c_values[:-1]], 0)
    ends = propagate(starts, diffusivity, velocity)
    residual = ends - c_values
    error = jnp.zeros_like(initial)
    product = jnp.ones_like(initial)
    for index_k in range(count):
        error = gains[index_k] * error + residual[index_k]
        product = product * gains[index_k]
    identity = (jnp.ones_like(initial), jnp.zeros_like(initial))
    entering = entering_2((product, error), "tm", combine_maps, identity)
    error = entering[1]
    results = []
    for index_k in range(count):
        error = gains[index_k] * error + residual[index_k]
        results.append(c_values[index_k] + error)
    return jnp.stack(results, 0)


def fused_kernel(
    n, nx, half,
    c_hbm, init_hbm, diff_hbm, vel_hbm, gains_hbm, out_ref,
    c_own, g_own, raw, coef, first, second, spare, ends,
    base, cum, block_e, all_p, all_e, leave, enter, below, above,
    local_sem, swap_send, swap_recv, start_send, start_recv, ends_send, ends_recv,
    p_send, p_recv, e_send, e_recv, x_send, x_recv, up_send, up_recv,
):
    t, s = lax.axis_index("tm"), lax.axis_index("slab")
    other = 1 - s
    lanes = c_own.shape[-1]
    planes = half // nx
    whole = 2 * half
    part = half // GROUP
    member = lax.rem(t, GROUP)
    leader = t - member
    mine = pl.ds(pl.multiple_of(s * half, half), half)
    theirs = pl.ds(pl.multiple_of(other * half, half), half)
    mine_in = pl.ds(pl.multiple_of(nx + s * half, nx), half)
    theirs_in = pl.ds(pl.multiple_of(nx + other * half, nx), half)

    barrier = pltpu.get_barrier_semaphore()

    def greet(where):
        pl.semaphore_signal(barrier, inc=1, device_id=where, device_id_type=MESH)

    zero = jnp.zeros((nx, lanes), jnp.float32)
    for field in (first, second, spare):
        field[0:nx] = zero
        field[nx + whole : 2 * nx + whole] = zero

    greet((t, other))
    for d in range(1, GROUP):
        greet((leader + lax.rem(member + d, GROUP), s))

    @pl.when(t >= GROUP)
    def _():
        greet((t - GROUP, s))

    @pl.when((s == 0) & (t > 0))
    def _():
        greet((t - 1, 1))

    @pl.when((s == 0) & (t > 0) & (member == 0))
    def _():
        greet((t - 1, 0))

    local_diff = pltpu.make_async_copy(diff_hbm, raw.at[0, mine], local_sem.at[0])
    local_vel = pltpu.make_async_copy(vel_hbm, raw.at[1:4, mine], local_sem.at[1])
    local_c = pltpu.make_async_copy(c_hbm, c_own, local_sem.at[2])
    local_g = pltpu.make_async_copy(gains_hbm, g_own, local_sem.at[3])
    local_first = pltpu.make_async_copy(c_hbm.at[2 * s], first.at[mine_in], local_sem.at[4])
    local_second = pltpu.make_async_copy(c_hbm.at[1], second.at[mine_in], local_sem.at[5])
    local_init = pltpu.make_async_copy(init_hbm, second.at[mine_in], local_sem.at[6])
    local_diff.start()
    local_vel.start()
    local_first.start()

    @pl.when(s == 1)
    def _():
        local_second.start()

    @pl.when((s == 0) & (t == 0))
    def _():
        local_init.start()

    local_g.start()
    local_c.start()

    later = jnp.where(t < n - GROUP, 1, 0)
    following = jnp.where((t < n - 1) & ((s == 1) | (member == GROUP - 1)), 1, 0)

    def remote(src, dst, send, recv, where):
        return pltpu.make_async_remote_copy(
            src_ref=src, dst_ref=dst, send_sem=send, recv_sem=recv,
            device_id=where, device_id_type=MESH,
        )

    swap_first = remote(
        c_hbm.at[2 * other], first.at[mine_in], swap_send.at[0], swap_recv.at[0], (t, other)
    )
    swap_diff = remote(diff_hbm, raw.at[0, mine], swap_send.at[1], swap_recv.at[1], (t, other))
    swap_vel = remote(vel_hbm, raw.at[1:4, mine], swap_send.at[2], swap_recv.at[2], (t, other))
    to_next = remote(
        c_hbm.at[3], second.at[mine_in], start_send.at[0], start_recv.at[s], (t + 1, 0)
    )
    to_upper = remote(
        c_hbm.at[1], second.at[mine_in], start_send.at[1], start_recv.at[s], (t, 1)
    )
    to_lower = remote(
        init_hbm, second.at[mine_in], start_send.at[2], start_recv.at[s], (t, 0)
    )

    row = lax.broadcasted_iota(jnp.int32, (nx, lanes), 0)
    lane = lax.broadcasted_iota(jnp.int32, (nx, lanes), 1)

    def coefficients(start):
        def plane(z, carry):
            at = pl.ds(pl.multiple_of(start + z * nx, nx), nx)
            d = raw[0, at]
            centre = 1.0 - 6.0 * d
            for q in range(3):
                speed = raw[q + 1, at]
                up = jnp.maximum(speed, 0.0)
                down = jnp.minimum(speed, 0.0)
                centre = centre - up + down
                minus = d + up
                plus = d - down
                if q == 1:
                    minus = jnp.where(row == 0, 0.0, minus)
                    plus = jnp.where(row == nx - 1, 0.0, plus)
                if q == 2:
                    minus = jnp.where(lane == 0, 0.0, minus)
                    plus = jnp.where(lane == lanes - 1, 0.0, plus)
                coef[1 + 2 * q, at] = minus
                coef[2 + 2 * q, at] = plus
            coef[0, at] = centre
            return carry

        lax.fori_loop(0, planes, plane, 0)

    local_diff.wait()
    local_vel.wait()
    coefficients(s * half)

    local_g.wait()

    def products(z, carry):
        at = pl.ds(pl.multiple_of(z * nx, nx), nx)
        p = g_own[0, at]
        cum[0, at] = p
        for k in range(1, 4):
            p = p * g_own[k, at]
            cum[k, at] = p
        return carry

    lax.fori_loop(0, planes, products, 0)

    pl.semaphore_wait(barrier, GROUP + later + following)

    @pl.when(t < n - 1)
    def _():
        to_next.start()

    swap_diff.start()
    swap_vel.start()
    swap_first.start()

    @pl.when(s == 0)
    def _():
        to_upper.start()

    @pl.when((s == 1) & (t == 0))
    def _():
        to_lower.start()

    def share(q):
        return pl.ds(pl.multiple_of(q * part, part), part)

    def p_copy(d):
        peer = lax.rem(member + d, GROUP)
        return remote(
            cum.at[3, share(peer)], all_p.at[member], p_send.at[d], p_recv.at[member],
            (leader + peer, s),
        )

    def e_copy(d):
        peer = lax.rem(member + d, GROUP)
        return remote(
            block_e.at[share(peer)], all_e.at[member], e_send.at[d], e_recv.at[member],
            (leader + peer, s),
        )

    def x_copy(peer):
        return remote(
            leave.at[peer], enter.at[share(member)], x_send.at[peer], x_recv.at[member],
            (leader + peer, s),
        )

    up = remote(above, below, up_send.at[0], up_recv.at[0], (t + GROUP, s))
    for d in range(1, GROUP):
        p_copy(d).start()

    swap_diff.wait_recv()
    swap_vel.wait_recv()
    coefficients(other * half)

    def step(src, dst):
        for z in range(2 * planes):
            at = nx + z * nx
            here = z * nx
            v = src[at : at + nx]
            new = coef[0, here : here + nx] * v
            new += coef[1, here : here + nx] * src[at - nx : at]
            new += coef[2, here : here + nx] * src[at + nx : at + 2 * nx]
            new += coef[3, here : here + nx] * src[at - 1 : at + nx - 1]
            new += coef[4, here : here + nx] * src[at + 1 : at + nx + 1]
            new += coef[5, here : here + nx] * pltpu.roll(v, 1, 1)
            new += coef[6, here : here + nx] * pltpu.roll(v, lanes - 1, 1)
            dst[at : at + nx] = new

    def propagated(field):
        def pair(i, carry):
            step(field, spare)
            step(spare, field)
            return carry

        lax.fori_loop(0, STEPS // 2, pair, 0)

    local_first.wait()
    swap_first.wait_recv()
    propagated(first)

    back_first = remote(
        first.at[theirs_in], ends.at[1], ends_send.at[0], ends_recv.at[0], (t, other)
    )
    back_first.start()

    @pl.when(s == 1)
    def _():
        local_second.wait()

    @pl.when((s == 0) & (t == 0))
    def _():
        local_init.wait()

    @pl.when((s == 1) | (t > 0))
    def _():
        remote(
            c_hbm.at[3], second.at[nx : nx + half], start_send.at[0], start_recv.at[0], (t, other)
        ).wait_recv()

    @pl.when(s == 0)
    def _():
        remote(
            c_hbm.at[3], second.at[nx + half : nx + whole],
            start_send.at[0], start_recv.at[1], (t, other),
        ).wait_recv()

    propagated(second)
    back_second = remote(
        second.at[theirs_in], ends.at[0], ends_send.at[1], ends_recv.at[1], (t, other)
    )
    back_second.start()
    local_c.wait()
    back_first.wait_recv()
    back_second.wait_recv()

    def local_errors(lower):
        def plane(z, carry):
            at = pl.ds(pl.multiple_of(z * nx, nx), nx)
            own_at = pl.ds(pl.multiple_of(nx + s * half + z * nx, nx), nx)
            own = [second[own_at], first[own_at]]
            got = [ends[0, at], ends[1, at]]
            finals = own + got if lower else got + own
            error = jnp.zeros((nx, lanes), jnp.float32)
            for k in range(4):
                c = c_own[k, at]
                error = g_own[k, at] * error + (finals[k] - c)
                base[k, at] = error + c
            block_e[at] = error
            return carry

        lax.fori_loop(0, planes, plane, 0)

    @pl.when(s == 0)
    def _():
        local_errors(True)

    @pl.when(s == 1)
    def _():
        local_errors(False)

    for d in range(1, GROUP):
        e_copy(d).start()
    all_p[member] = cum[3, share(member)]
    all_e[member] = block_e[share(member)]
    for i in range(GROUP):
        @pl.when(i != member)
        def _():
            remote(
                cum.at[3, share(i)], all_p.at[i], p_send.at[0], p_recv.at[i], (leader + i, s)
            ).wait_recv()
            remote(
                block_e.at[share(i)], all_e.at[i], e_send.at[0], e_recv.at[i], (leader + i, s)
            ).wait_recv()

    total = all_e[0]
    product = all_p[0]
    for i in range(1, GROUP):
        total = all_p[i] * total + all_e[i]
        product = all_p[i] * product

    @pl.when(t < GROUP)
    def _():
        leave[0] = jnp.zeros((part, lanes), jnp.float32)

    @pl.when(t >= GROUP)
    def _():
        remote(above, below, up_send.at[0], up_recv.at[0], (leader, other)).wait_recv()
        leave[0] = below[...]

    above[...] = product * leave[0] + total

    @pl.when(t < n - GROUP)
    def _():
        up.start()

    for i in range(GROUP):
        if i:
            leave[i] = all_p[i - 1] * leave[i - 1] + all_e[i - 1]

        @pl.when(i != member)
        def _():
            x_copy(i).start()

    enter[share(member)] = leave[member]

    def finish(d, carry):
        q = lax.rem(member + d, GROUP)

        @pl.when(d > 0)
        def _():
            remote(
                leave.at[q], enter.at[share(q)], x_send.at[q], x_recv.at[q], (leader + q, s)
            ).wait_recv()

        at = share(q)
        entering = enter[at]
        for k in range(4):
            out_ref[k, at] = base[k, at] + cum[k, at] * entering
        return carry

    lax.fori_loop(0, GROUP, finish, 0)

    swap_first.wait_send()
    swap_diff.wait_send()
    swap_vel.wait_send()

    @pl.when(t < n - 1)
    def _():
        to_next.wait_send()

    @pl.when(s == 0)
    def _():
        to_upper.wait_send()

    @pl.when((s == 1) & (t == 0))
    def _():
        to_lower.wait_send()

    back_first.wait_send()
    back_second.wait_send()

    for d in range(1, GROUP):
        p_copy(d).wait_send()
        e_copy(d).wait_send()
        x_copy(lax.rem(member + d, GROUP)).wait_send()

    @pl.when(t < n - GROUP)
    def _():
        up.wait_send()


def fused(c_values, initial, diffusivity, velocity, gains):
    n = lax.axis_size("tm")
    count, nz, nx, ny = c_values.shape
    half = nz * nx
    part = half // GROUP
    f32 = jnp.float32
    dma = pltpu.SemaphoreType.DMA
    field = pltpu.VMEM((2 * half + 2 * nx, ny), f32)
    block = pltpu.VMEM((half, ny), f32)
    four = pltpu.VMEM((4, half, ny), f32)
    shares = pltpu.VMEM((GROUP, part, ny), f32)
    share = pltpu.VMEM((part, ny), f32)
    out = pl.pallas_call(
        functools.partial(fused_kernel, n, nx, half),
        out_shape=jax.ShapeDtypeStruct((count, half, ny), f32),
        in_specs=[pl.BlockSpec(memory_space=pltpu.HBM)] * 5,
        out_specs=pl.BlockSpec(memory_space=pltpu.VMEM),
        scratch_shapes=[
            four, four,
            pltpu.VMEM((4, 2 * half, ny), f32),
            pltpu.VMEM((7, 2 * half, ny), f32),
            field, field, field,
            pltpu.VMEM((2, half, ny), f32),
            four, four, block, shares, shares, shares, block, share, share,
            dma((7,)), dma((3,)), dma((3,)), dma((3,)), dma((2,)), dma((2,)), dma((2,)),
            dma((GROUP,)), dma((GROUP,)), dma((GROUP,)), dma((GROUP,)), dma((GROUP,)), dma((GROUP,)),
            dma((1,)), dma((1,)),
        ],
        compiler_params=pltpu.CompilerParams(
            collective_id=0, has_side_effects=True, vmem_limit_bytes=60 * 1024 * 1024
        ),
    )(
        c_values.reshape(count, half, ny),
        initial.reshape(half, ny),
        diffusivity.reshape(half, ny),
        velocity.reshape(3, half, ny),
        gains.reshape(count, half, ny),
    )
    return out.reshape(c_values.shape)


def planned(c_values, initial, diffusivity, velocity, gains):
    n, slabs = lax.axis_size("tm"), lax.axis_size("slab")
    count, nz, nx, ny = c_values.shape
    fits = slabs == 2 and count == 4 and n % GROUP == 0 and nx % 8 == 0 and ny % 128 == 0
    if fits and (nz * nx) % (8 * GROUP) == 0:
        return fused(c_values, initial, diffusivity, velocity, gains)
    return body(c_values, initial, diffusivity, velocity, gains)


def solution(mesh):
    placed = (
        P("tm", "slab", None, None),
        P("slab", None, None),
        P("slab", None, None),
        P(None, "slab", None, None),
        P("tm", "slab", None, None),
    )
    return jax.shard_map(
        planned, mesh=mesh, in_specs=placed, out_specs=P("tm", "slab", None, None), check_vma=False
    )
```

```python
import functools

import jax
import jax.numpy as jnp
from jax import lax
from jax.experimental import pallas as pl
from jax.experimental.pallas import tpu as pltpu
from jax.sharding import PartitionSpec as P

STEPS = 8
GROUP = 4
MESH = pl.DeviceIdType.MESH


def padded_2(block, sides, width):
    for axis, dim in sides:
        count = lax.axis_size(axis)
        forward = [(i, i + 1) for i in range(count - 1)]
        backward = [(target, source) for source, target in forward]
        low = lax.ppermute(
            lax.slice_in_dim(block, block.shape[dim] - width, None, axis=dim), axis, forward
        )
        high = lax.ppermute(lax.slice_in_dim(block, 0, width, axis=dim), axis, backward)
        block = jnp.concatenate([low, block, high], axis=dim)
    return block


def shifted(value, axis, steps):
    count = lax.axis_size(axis)
    first, last = (max(0, -steps), min(count, count - steps))
    return lax.ppermute(value, axis, [(source, source + steps) for source in range(first, last)])


def entering_2(part, axis, combine, identity):
    place = lax.axis_index(axis)
    gathered = jax.tree.map(lambda a: lax.all_gather(a, axis), part)
    state = jax.tree.map(lambda a, e: jnp.zeros_like(a) + jnp.asarray(e, a.dtype), part, identity)

    def one(step, state):
        return combine(
            state, jax.tree.map(lambda a: lax.dynamic_index_in_dim(a, step, 0, False), gathered)
        )

    return lax.fori_loop(0, place, one, state)


def upwind(speed, center, minus, plus):
    return jnp.maximum(speed, 0.0) * (center - minus) + jnp.minimum(speed, 0.0) * (plus - center)


def advance(padded, diffusivity, velocity):
    center = padded[:, 1:-1]
    lower_z = padded[:, :-2]
    upper_z = padded[:, 2:]
    flat = jnp.pad(center, ((0, 0), (0, 0), (1, 1), (1, 1)))
    lower_x = flat[:, :, :-2, 1:-1]
    upper_x = flat[:, :, 2:, 1:-1]
    lower_y = flat[:, :, 1:-1, :-2]
    upper_y = flat[:, :, 1:-1, 2:]
    laplace = lower_z + upper_z + lower_x + upper_x + lower_y + upper_y - 6.0 * center
    transport = (
        upwind(velocity[0], center, lower_z, upper_z)
        + upwind(velocity[1], center, lower_x, upper_x)
        + upwind(velocity[2], center, lower_y, upper_y)
    )
    return center + diffusivity * laplace - transport


def propagate(field, diffusivity, velocity):
    for step in range(STEPS):
        padded = padded_2(field, (("slab", 1),), 1)
        field = advance(padded, diffusivity, velocity)
    return field


def combine_maps(earlier, later):
    return (earlier[0] * later[0], later[0] * earlier[1] + later[1])


def body(c_values, initial, diffusivity, velocity, gains):
    count = c_values.shape[0]
    is_first = lax.axis_index("tm") == 0
    received = shifted(c_values[-1], "tm", 1)
    previous = jnp.where(is_first, initial, received)
    starts = jnp.concatenate([previous[None], c_values[:-1]], 0)
    ends = propagate(starts, diffusivity, velocity)
    residual = ends - c_values
    error = jnp.zeros_like(initial)
    product = jnp.ones_like(initial)
    for index_k in range(count):
        error = gains[index_k] * error + residual[index_k]
        product = product * gains[index_k]
    identity = (jnp.ones_like(initial), jnp.zeros_like(initial))
    entering = entering_2((product, error), "tm", combine_maps, identity)
    error = entering[1]
    results = []
    for index_k in range(count):
        error = gains[index_k] * error + residual[index_k]
        results.append(c_values[index_k] + error)
    return jnp.stack(results, 0)


def fused_kernel(
    n, nx, half,
    c_hbm, init_hbm, diff_hbm, vel_hbm, gains_hbm, out_ref,
    c_own, g_own, raw, coef, first, second, spare, ends,
    base, cum, block_e, all_p, all_e, leave, enter, below_p, below_e, group_p, group_e,
    local_sem, swap_send, swap_recv, start_send, start_recv, ends_send, ends_recv,
    p_send, p_recv, e_send, e_recv, x_send, x_recv, up_send, up_recv, q_send, q_recv,
):
    t, s = lax.axis_index("tm"), lax.axis_index("slab")
    other = 1 - s
    lanes = c_own.shape[-1]
    planes = half // nx
    whole = 2 * half
    part = half // GROUP
    member = lax.rem(t, GROUP)
    leader = t - member
    groups = n // GROUP
    group = t // GROUP
    mine = pl.ds(pl.multiple_of(s * half, half), half)
    theirs = pl.ds(pl.multiple_of(other * half, half), half)
    mine_in = pl.ds(pl.multiple_of(nx + s * half, nx), half)
    theirs_in = pl.ds(pl.multiple_of(nx + other * half, nx), half)

    barrier = pltpu.get_barrier_semaphore()

    def greet(where):
        pl.semaphore_signal(barrier, inc=1, device_id=where, device_id_type=MESH)

    zero = jnp.zeros((nx, lanes), jnp.float32)
    for field in (first, second, spare):
        field[0:nx] = zero
        field[nx + whole : 2 * nx + whole] = zero

    greet((t, other))
    for d in range(1, GROUP):
        greet((leader + lax.rem(member + d, GROUP), s))

    for i in range(groups):
        @pl.when(i < group)
        def _():
            greet((i * GROUP + member, s))

    @pl.when((s == 0) & (t > 0))
    def _():
        greet((t - 1, 1))

    @pl.when((s == 0) & (t > 0) & (member == 0))
    def _():
        greet((t - 1, 0))

    local_diff = pltpu.make_async_copy(diff_hbm, raw.at[0, mine], local_sem.at[0])
    local_vel = pltpu.make_async_copy(vel_hbm, raw.at[1:4, mine], local_sem.at[1])
    local_c = pltpu.make_async_copy(c_hbm, c_own, local_sem.at[2])
    local_g = pltpu.make_async_copy(gains_hbm, g_own, local_sem.at[3])
    local_first = pltpu.make_async_copy(c_hbm.at[2 * s], first.at[mine_in], local_sem.at[4])
    local_second = pltpu.make_async_copy(c_hbm.at[1], second.at[mine_in], local_sem.at[5])
    local_init = pltpu.make_async_copy(init_hbm, second.at[mine_in], local_sem.at[6])
    local_diff.start()
    local_vel.start()
    local_first.start()

    @pl.when(s == 1)
    def _():
        local_second.start()

    @pl.when((s == 0) & (t == 0))
    def _():
        local_init.start()

    local_g.start()
    local_c.start()

    later = groups - 1 - group
    following = jnp.where((t < n - 1) & ((s == 1) | (member == GROUP - 1)), 1, 0)

    def remote(src, dst, send, recv, where):
        return pltpu.make_async_remote_copy(
            src_ref=src, dst_ref=dst, send_sem=send, recv_sem=recv,
            device_id=where, device_id_type=MESH,
        )

    swap_first = remote(
        c_hbm.at[2 * other], first.at[mine_in], swap_send.at[0], swap_recv.at[0], (t, other)
    )
    swap_diff = remote(diff_hbm, raw.at[0, mine], swap_send.at[1], swap_recv.at[1], (t, other))
    swap_vel = remote(vel_hbm, raw.at[1:4, mine], swap_send.at[2], swap_recv.at[2], (t, other))
    to_next = remote(
        c_hbm.at[3], second.at[mine_in], start_send.at[0], start_recv.at[s], (t + 1, 0)
    )
    to_upper = remote(
        c_hbm.at[1], second.at[mine_in], start_send.at[1], start_recv.at[s], (t, 1)
    )
    to_lower = remote(
        init_hbm, second.at[mine_in], start_send.at[2], start_recv.at[s], (t, 0)
    )

    row = lax.broadcasted_iota(jnp.int32, (nx, lanes), 0)
    lane = lax.broadcasted_iota(jnp.int32, (nx, lanes), 1)

    def coefficients(start):
        def plane(z, carry):
            at = pl.ds(pl.multiple_of(start + z * nx, nx), nx)
            d = raw[0, at]
            centre = 1.0 - 6.0 * d
            for q in range(3):
                speed = raw[q + 1, at]
                up = jnp.maximum(speed, 0.0)
                down = jnp.minimum(speed, 0.0)
                centre = centre - up + down
                minus = d + up
                plus = d - down
                if q == 1:
                    minus = jnp.where(row == 0, 0.0, minus)
                    plus = jnp.where(row == nx - 1, 0.0, plus)
                if q == 2:
                    minus = jnp.where(lane == 0, 0.0, minus)
                    plus = jnp.where(lane == lanes - 1, 0.0, plus)
                coef[1 + 2 * q, at] = minus
                coef[2 + 2 * q, at] = plus
            coef[0, at] = centre
            return carry

        lax.fori_loop(0, planes, plane, 0)

    local_diff.wait()
    local_vel.wait()
    coefficients(s * half)

    local_g.wait()

    def products(z, carry):
        at = pl.ds(pl.multiple_of(z * nx, nx), nx)
        p = g_own[0, at]
        cum[0, at] = p
        for k in range(1, 4):
            p = p * g_own[k, at]
            cum[k, at] = p
        return carry

    lax.fori_loop(0, planes, products, 0)

    pl.semaphore_wait(barrier, GROUP + later + following)

    @pl.when(t < n - 1)
    def _():
        to_next.start()

    swap_diff.start()
    swap_vel.start()
    swap_first.start()

    @pl.when(s == 0)
    def _():
        to_upper.start()

    @pl.when((s == 1) & (t == 0))
    def _():
        to_lower.start()

    def share(q):
        return pl.ds(pl.multiple_of(q * part, part), part)

    def p_copy(d):
        peer = lax.rem(member + d, GROUP)
        return remote(
            cum.at[3, share(peer)], all_p.at[member], p_send.at[d], p_recv.at[member],
            (leader + peer, s),
        )

    def e_copy(d):
        peer = lax.rem(member + d, GROUP)
        return remote(
            block_e.at[share(peer)], all_e.at[member], e_send.at[d], e_recv.at[member],
            (leader + peer, s),
        )

    def x_copy(peer):
        return remote(
            leave.at[peer], enter.at[share(member)], x_send.at[peer], x_recv.at[member],
            (leader + peer, s),
        )

    def q_copy(i):
        return remote(
            group_p, below_p.at[group], q_send.at[i], q_recv.at[group], (i * GROUP + member, s)
        )

    def up_copy(i):
        return remote(
            group_e, below_e.at[group], up_send.at[i], up_recv.at[group], (i * GROUP + member, s)
        )

    def to_later(act):
        for i in range(1, groups):
            @pl.when(i > group)
            def _():
                act(i)

    swap_diff.wait_recv()
    swap_vel.wait_recv()
    coefficients(other * half)

    def step(src, dst):
        for z in range(2 * planes):
            at = nx + z * nx
            here = z * nx
            v = src[at : at + nx]
            new = coef[0, here : here + nx] * v
            new += coef[1, here : here + nx] * src[at - nx : at]
            new += coef[2, here : here + nx] * src[at + nx : at + 2 * nx]
            new += coef[3, here : here + nx] * src[at - 1 : at + nx - 1]
            new += coef[4, here : here + nx] * src[at + 1 : at + nx + 1]
            new += coef[5, here : here + nx] * pltpu.roll(v, 1, 1)
            new += coef[6, here : here + nx] * pltpu.roll(v, lanes - 1, 1)
            dst[at : at + nx] = new

    def propagated(field):
        def pair(i, carry):
            step(field, spare)
            step(spare, field)
            return carry

        lax.fori_loop(0, STEPS // 2, pair, 0)

    local_first.wait()
    swap_first.wait_recv()
    propagated(first)
    for d in range(1, GROUP):
        p_copy(d).start()

    back_first = remote(
        first.at[theirs_in], ends.at[1], ends_send.at[0], ends_recv.at[0], (t, other)
    )
    back_first.start()

    @pl.when(s == 1)
    def _():
        local_second.wait()

    @pl.when((s == 0) & (t == 0))
    def _():
        local_init.wait()

    @pl.when((s == 1) | (t > 0))
    def _():
        remote(
            c_hbm.at[3], second.at[nx : nx + half], start_send.at[0], start_recv.at[0], (t, other)
        ).wait_recv()

    @pl.when(s == 0)
    def _():
        remote(
            c_hbm.at[3], second.at[nx + half : nx + whole],
            start_send.at[0], start_recv.at[1], (t, other),
        ).wait_recv()

    propagated(second)
    back_second = remote(
        second.at[theirs_in], ends.at[0], ends_send.at[1], ends_recv.at[1], (t, other)
    )
    back_second.start()
    local_c.wait()
    all_p[member] = cum[3, share(member)]
    for i in range(GROUP):
        @pl.when(i != member)
        def _():
            remote(
                cum.at[3, share(i)], all_p.at[i], p_send.at[0], p_recv.at[i], (leader + i, s)
            ).wait_recv()

    product = all_p[0]
    for i in range(1, GROUP):
        product = all_p[i] * product
    group_p[...] = product
    to_later(lambda i: q_copy(i).start())
    back_first.wait_recv()
    back_second.wait_recv()

    def local_errors(lower):
        def plane(z, carry):
            at = pl.ds(pl.multiple_of(z * nx, nx), nx)
            own_at = pl.ds(pl.multiple_of(nx + s * half + z * nx, nx), nx)
            own = [second[own_at], first[own_at]]
            got = [ends[0, at], ends[1, at]]
            finals = own + got if lower else got + own
            error = jnp.zeros((nx, lanes), jnp.float32)
            for k in range(4):
                c = c_own[k, at]
                error = g_own[k, at] * error + (finals[k] - c)
                base[k, at] = error
            block_e[at] = error
            return carry

        lax.fori_loop(0, planes, plane, 0)

    @pl.when(s == 0)
    def _():
        local_errors(True)

    @pl.when(s == 1)
    def _():
        local_errors(False)

    for d in range(1, GROUP):
        e_copy(d).start()
    all_e[member] = block_e[share(member)]
    for i in range(GROUP):
        @pl.when(i != member)
        def _():
            remote(
                block_e.at[share(i)], all_e.at[i], e_send.at[0], e_recv.at[i], (leader + i, s)
            ).wait_recv()

    total = all_e[0]
    for i in range(1, GROUP):
        total = all_p[i] * total + all_e[i]
    group_e[...] = total
    to_later(lambda i: up_copy(i).start())
    leave[0] = jnp.zeros((part, lanes), jnp.float32)
    for i in range(groups - 1):
        @pl.when(i < group)
        def _():
            remote(
                group_p, below_p.at[i], q_send.at[0], q_recv.at[i], (i * GROUP + member, s)
            ).wait_recv()
            remote(
                group_e, below_e.at[i], up_send.at[0], up_recv.at[i], (i * GROUP + member, s)
            ).wait_recv()
            leave[0] = below_p[i] * leave[0] + below_e[i]

    for i in range(GROUP):
        if i:
            leave[i] = all_p[i - 1] * leave[i - 1] + all_e[i - 1]

        @pl.when(i != member)
        def _():
            x_copy(i).start()

    enter[share(member)] = leave[member]

    def finish(d, carry):
        q = lax.rem(member + d, GROUP)

        @pl.when(d > 0)
        def _():
            remote(
                leave.at[q], enter.at[share(q)], x_send.at[q], x_recv.at[q], (leader + q, s)
            ).wait_recv()

        at = share(q)
        entering = enter[at]
        for k in range(4):
            out_ref[k, at] = base[k, at] + cum[k, at] * entering
        return carry

    lax.fori_loop(0, GROUP, finish, 0)

    swap_first.wait_send()
    swap_diff.wait_send()
    swap_vel.wait_send()

    @pl.when(t < n - 1)
    def _():
        to_next.wait_send()

    @pl.when(s == 0)
    def _():
        to_upper.wait_send()

    @pl.when((s == 1) & (t == 0))
    def _():
        to_lower.wait_send()

    back_first.wait_send()
    back_second.wait_send()

    for d in range(1, GROUP):
        p_copy(d).wait_send()
        e_copy(d).wait_send()
        x_copy(lax.rem(member + d, GROUP)).wait_send()

    to_later(lambda i: q_copy(i).wait_send())
    to_later(lambda i: up_copy(i).wait_send())


def fused(c_values, initial, diffusivity, velocity, gains):
    n = lax.axis_size("tm")
    count, nz, nx, ny = c_values.shape
    half = nz * nx
    part = half // GROUP
    f32 = jnp.float32
    dma = pltpu.SemaphoreType.DMA
    field = pltpu.VMEM((2 * half + 2 * nx, ny), f32)
    block = pltpu.VMEM((half, ny), f32)
    four = pltpu.VMEM((4, half, ny), f32)
    shares = pltpu.VMEM((GROUP, part, ny), f32)
    share = pltpu.VMEM((part, ny), f32)
    groups = n // GROUP
    belows = pltpu.VMEM((groups, part, ny), f32)
    error = pl.pallas_call(
        functools.partial(fused_kernel, n, nx, half),
        out_shape=jax.ShapeDtypeStruct((count, half, ny), f32),
        in_specs=[pl.BlockSpec(memory_space=pltpu.HBM)] * 5,
        out_specs=pl.BlockSpec(memory_space=pltpu.VMEM),
        scratch_shapes=[
            four, four,
            pltpu.VMEM((4, 2 * half, ny), f32),
            pltpu.VMEM((7, 2 * half, ny), f32),
            field, field, field,
            pltpu.VMEM((2, half, ny), f32),
            four, four, block, shares, shares, shares, block, belows, belows, share, share,
            dma((7,)), dma((3,)), dma((3,)), dma((3,)), dma((2,)), dma((2,)), dma((2,)),
            dma((GROUP,)), dma((GROUP,)), dma((GROUP,)), dma((GROUP,)), dma((GROUP,)), dma((GROUP,)),
            dma((groups,)), dma((groups,)), dma((groups,)), dma((groups,)),
        ],
        compiler_params=pltpu.CompilerParams(
            collective_id=0, has_side_effects=True, vmem_limit_bytes=60 * 1024 * 1024
        ),
    )(
        c_values.reshape(count, half, ny),
        initial.reshape(half, ny),
        diffusivity.reshape(half, ny),
        velocity.reshape(3, half, ny),
        gains.reshape(count, half, ny),
    )
    return c_values + error.reshape(c_values.shape)


def planned(c_values, initial, diffusivity, velocity, gains):
    n, slabs = lax.axis_size("tm"), lax.axis_size("slab")
    count, nz, nx, ny = c_values.shape
    fits = slabs == 2 and count == 4 and n % GROUP == 0 and nx % 8 == 0 and ny % 128 == 0
    if fits and (nz * nx) % (8 * GROUP) == 0:
        return fused(c_values, initial, diffusivity, velocity, gains)
    return body(c_values, initial, diffusivity, velocity, gains)


def solution(mesh):
    placed = (
        P("tm", "slab", None, None),
        P("slab", None, None),
        P("slab", None, None),
        P(None, "slab", None, None),
        P("tm", "slab", None, None),
    )
    return jax.shard_map(
        planned, mesh=mesh, in_specs=placed, out_specs=P("tm", "slab", None, None), check_vma=False
    )
```

```python
import functools

import jax
import jax.numpy as jnp
from jax import lax
from jax.experimental import pallas as pl
from jax.experimental.pallas import tpu as pltpu
from jax.sharding import PartitionSpec as P

STEPS = 8
GROUP = 4
MESH = pl.DeviceIdType.MESH


def padded_2(block, sides, width):
    for axis, dim in sides:
        count = lax.axis_size(axis)
        forward = [(i, i + 1) for i in range(count - 1)]
        backward = [(target, source) for source, target in forward]
        low = lax.ppermute(
            lax.slice_in_dim(block, block.shape[dim] - width, None, axis=dim), axis, forward
        )
        high = lax.ppermute(lax.slice_in_dim(block, 0, width, axis=dim), axis, backward)
        block = jnp.concatenate([low, block, high], axis=dim)
    return block


def shifted(value, axis, steps):
    count = lax.axis_size(axis)
    first, last = (max(0, -steps), min(count, count - steps))
    return lax.ppermute(value, axis, [(source, source + steps) for source in range(first, last)])


def entering_2(part, axis, combine, identity):
    place = lax.axis_index(axis)
    gathered = jax.tree.map(lambda a: lax.all_gather(a, axis), part)
    state = jax.tree.map(lambda a, e: jnp.zeros_like(a) + jnp.asarray(e, a.dtype), part, identity)

    def one(step, state):
        return combine(
            state, jax.tree.map(lambda a: lax.dynamic_index_in_dim(a, step, 0, False), gathered)
        )

    return lax.fori_loop(0, place, one, state)


def upwind(speed, center, minus, plus):
    return jnp.maximum(speed, 0.0) * (center - minus) + jnp.minimum(speed, 0.0) * (plus - center)


def advance(padded, diffusivity, velocity):
    center = padded[:, 1:-1]
    lower_z = padded[:, :-2]
    upper_z = padded[:, 2:]
    flat = jnp.pad(center, ((0, 0), (0, 0), (1, 1), (1, 1)))
    lower_x = flat[:, :, :-2, 1:-1]
    upper_x = flat[:, :, 2:, 1:-1]
    lower_y = flat[:, :, 1:-1, :-2]
    upper_y = flat[:, :, 1:-1, 2:]
    laplace = lower_z + upper_z + lower_x + upper_x + lower_y + upper_y - 6.0 * center
    transport = (
        upwind(velocity[0], center, lower_z, upper_z)
        + upwind(velocity[1], center, lower_x, upper_x)
        + upwind(velocity[2], center, lower_y, upper_y)
    )
    return center + diffusivity * laplace - transport


def propagate(field, diffusivity, velocity):
    for step in range(STEPS):
        padded = padded_2(field, (("slab", 1),), 1)
        field = advance(padded, diffusivity, velocity)
    return field


def combine_maps(earlier, later):
    return (earlier[0] * later[0], later[0] * earlier[1] + later[1])


def body(c_values, initial, diffusivity, velocity, gains):
    count = c_values.shape[0]
    is_first = lax.axis_index("tm") == 0
    received = shifted(c_values[-1], "tm", 1)
    previous = jnp.where(is_first, initial, received)
    starts = jnp.concatenate([previous[None], c_values[:-1]], 0)
    ends = propagate(starts, diffusivity, velocity)
    residual = ends - c_values
    error = jnp.zeros_like(initial)
    product = jnp.ones_like(initial)
    for index_k in range(count):
        error = gains[index_k] * error + residual[index_k]
        product = product * gains[index_k]
    identity = (jnp.ones_like(initial), jnp.zeros_like(initial))
    entering = entering_2((product, error), "tm", combine_maps, identity)
    error = entering[1]
    results = []
    for index_k in range(count):
        error = gains[index_k] * error + residual[index_k]
        results.append(c_values[index_k] + error)
    return jnp.stack(results, 0)


def fused_kernel(
    n, nx, half,
    c_hbm, init_hbm, diff_hbm, vel_hbm, gains_hbm, out_ref,
    c_own, g_own, raw, coef, first, second, spare, ends,
    base, cum, block_e, all_p, all_e, leave, enter, below_p, below_e, group_p, group_e,
    local_sem, swap_send, swap_recv, start_send, start_recv, ends_send, ends_recv,
    p_send, p_recv, e_send, e_recv, x_send, x_recv, up_send, up_recv, q_send, q_recv,
):
    t, s = lax.axis_index("tm"), lax.axis_index("slab")
    other = 1 - s
    lanes = c_own.shape[-1]
    planes = half // nx
    whole = 2 * half
    part = half // GROUP
    member = lax.rem(t, GROUP)
    leader = t - member
    groups = n // GROUP
    group = t // GROUP
    mine = pl.ds(pl.multiple_of(s * half, half), half)
    theirs = pl.ds(pl.multiple_of(other * half, half), half)
    mine_in = pl.ds(pl.multiple_of(nx + s * half, nx), half)
    theirs_in = pl.ds(pl.multiple_of(nx + other * half, nx), half)

    barrier = pltpu.get_barrier_semaphore()

    def greet(where):
        pl.semaphore_signal(barrier, inc=1, device_id=where, device_id_type=MESH)

    zero = jnp.zeros((nx, lanes), jnp.float32)
    for field in (first, second, spare):
        field[0:nx] = zero
        field[nx + whole : 2 * nx + whole] = zero

    greet((t, other))
    for d in range(1, GROUP):
        greet((leader + lax.rem(member + d, GROUP), s))

    for i in range(groups):
        @pl.when(i < group)
        def _():
            greet((i * GROUP + member, s))

    @pl.when((s == 0) & (t > 0))
    def _():
        greet((t - 1, 1))

    @pl.when((s == 0) & (t > 0) & (member == 0))
    def _():
        greet((t - 1, 0))

    local_diff = pltpu.make_async_copy(diff_hbm, raw.at[0, mine], local_sem.at[0])
    local_vel = pltpu.make_async_copy(vel_hbm, raw.at[1:4, mine], local_sem.at[1])
    local_c = pltpu.make_async_copy(c_hbm, c_own, local_sem.at[2])
    local_g = pltpu.make_async_copy(gains_hbm, g_own, local_sem.at[3])
    local_first = pltpu.make_async_copy(c_hbm.at[2 * s], first.at[mine_in], local_sem.at[4])
    local_second = pltpu.make_async_copy(c_hbm.at[1], second.at[mine_in], local_sem.at[5])
    local_init = pltpu.make_async_copy(init_hbm, second.at[mine_in], local_sem.at[6])
    local_diff.start()
    local_vel.start()
    local_first.start()

    @pl.when(s == 1)
    def _():
        local_second.start()

    @pl.when((s == 0) & (t == 0))
    def _():
        local_init.start()

    local_g.start()
    local_c.start()

    later = groups - 1 - group
    following = jnp.where((t < n - 1) & ((s == 1) | (member == GROUP - 1)), 1, 0)

    def remote(src, dst, send, recv, where):
        return pltpu.make_async_remote_copy(
            src_ref=src, dst_ref=dst, send_sem=send, recv_sem=recv,
            device_id=where, device_id_type=MESH,
        )

    swap_first = remote(
        c_hbm.at[2 * other], first.at[mine_in], swap_send.at[0], swap_recv.at[0], (t, other)
    )
    swap_diff = remote(diff_hbm, raw.at[0, mine], swap_send.at[1], swap_recv.at[1], (t, other))
    swap_vel = remote(vel_hbm, raw.at[1:4, mine], swap_send.at[2], swap_recv.at[2], (t, other))
    to_next = remote(
        c_hbm.at[3], second.at[mine_in], start_send.at[0], start_recv.at[s], (t + 1, 0)
    )
    to_upper = remote(
        c_hbm.at[1], second.at[mine_in], start_send.at[1], start_recv.at[s], (t, 1)
    )
    to_lower = remote(
        init_hbm, second.at[mine_in], start_send.at[2], start_recv.at[s], (t, 0)
    )

    row = lax.broadcasted_iota(jnp.int32, (nx, lanes), 0)
    lane = lax.broadcasted_iota(jnp.int32, (nx, lanes), 1)

    def coefficients(start):
        def plane(z, carry):
            at = pl.ds(pl.multiple_of(start + z * nx, nx), nx)
            d = raw[0, at]
            centre = 1.0 - 6.0 * d
            for q in range(3):
                speed = raw[q + 1, at]
                up = jnp.maximum(speed, 0.0)
                down = jnp.minimum(speed, 0.0)
                centre = centre - up + down
                minus = d + up
                plus = d - down
                if q == 1:
                    minus = jnp.where(row == 0, 0.0, minus)
                    plus = jnp.where(row == nx - 1, 0.0, plus)
                if q == 2:
                    minus = jnp.where(lane == 0, 0.0, minus)
                    plus = jnp.where(lane == lanes - 1, 0.0, plus)
                coef[1 + 2 * q, at] = minus
                coef[2 + 2 * q, at] = plus
            coef[0, at] = centre
            return carry

        lax.fori_loop(0, planes, plane, 0)

    local_diff.wait()
    local_vel.wait()
    coefficients(s * half)

    local_g.wait()

    def products(z, carry):
        at = pl.ds(pl.multiple_of(z * nx, nx), nx)
        p = g_own[0, at]
        cum[0, at] = p
        for k in range(1, 4):
            p = p * g_own[k, at]
            cum[k, at] = p
        return carry

    lax.fori_loop(0, planes, products, 0)

    pl.semaphore_wait(barrier, GROUP + later + following)

    @pl.when(t < n - 1)
    def _():
        to_next.start()

    swap_diff.start()
    swap_vel.start()
    swap_first.start()

    @pl.when(s == 0)
    def _():
        to_upper.start()

    @pl.when((s == 1) & (t == 0))
    def _():
        to_lower.start()

    def share(q):
        return pl.ds(pl.multiple_of(q * part, part), part)

    def p_copy(d):
        peer = lax.rem(member + d, GROUP)
        return remote(
            cum.at[3, share(peer)], all_p.at[member], p_send.at[d], p_recv.at[member],
            (leader + peer, s),
        )

    def e_copy(d):
        peer = lax.rem(member + d, GROUP)
        return remote(
            block_e.at[share(peer)], all_e.at[member], e_send.at[d], e_recv.at[member],
            (leader + peer, s),
        )

    def x_copy(peer):
        return remote(
            leave.at[peer], enter.at[share(member)], x_send.at[peer], x_recv.at[member],
            (leader + peer, s),
        )

    def q_copy(i):
        return remote(
            group_p, below_p.at[group], q_send.at[i], q_recv.at[group], (i * GROUP + member, s)
        )

    def up_copy(i):
        return remote(
            group_e, below_e.at[group], up_send.at[i], up_recv.at[group], (i * GROUP + member, s)
        )

    def to_later(act):
        for i in range(1, groups):
            @pl.when(i > group)
            def _():
                act(i)

    swap_diff.wait_recv()
    swap_vel.wait_recv()
    coefficients(other * half)

    def step(src, dst):
        for z in range(2 * planes):
            at = nx + z * nx
            here = z * nx
            v = src[at : at + nx]
            new = coef[0, here : here + nx] * v
            new += coef[1, here : here + nx] * src[at - nx : at]
            new += coef[2, here : here + nx] * src[at + nx : at + 2 * nx]
            new += coef[3, here : here + nx] * src[at - 1 : at + nx - 1]
            new += coef[4, here : here + nx] * src[at + 1 : at + nx + 1]
            new += coef[5, here : here + nx] * pltpu.roll(v, 1, 1)
            new += coef[6, here : here + nx] * pltpu.roll(v, lanes - 1, 1)
            dst[at : at + nx] = new

    def propagated(field):
        def pair(i, carry):
            step(field, spare)
            step(spare, field)
            return carry

        lax.fori_loop(0, STEPS // 2, pair, 0)

    local_first.wait()
    swap_first.wait_recv()
    propagated(first)
    for d in range(1, GROUP):
        p_copy(d).start()

    back_first = remote(
        first.at[theirs_in], ends.at[1], ends_send.at[0], ends_recv.at[0], (t, other)
    )
    back_first.start()

    @pl.when(s == 1)
    def _():
        local_second.wait()

    @pl.when((s == 0) & (t == 0))
    def _():
        local_init.wait()

    @pl.when((s == 1) | (t > 0))
    def _():
        remote(
            c_hbm.at[3], second.at[nx : nx + half], start_send.at[0], start_recv.at[0], (t, other)
        ).wait_recv()

    @pl.when(s == 0)
    def _():
        remote(
            c_hbm.at[3], second.at[nx + half : nx + whole],
            start_send.at[0], start_recv.at[1], (t, other),
        ).wait_recv()

    propagated(second)
    back_second = remote(
        second.at[theirs_in], ends.at[0], ends_send.at[1], ends_recv.at[1], (t, other)
    )
    back_second.start()
    local_c.wait()
    all_p[member] = cum[3, share(member)]
    for i in range(GROUP):
        @pl.when(i != member)
        def _():
            remote(
                cum.at[3, share(i)], all_p.at[i], p_send.at[0], p_recv.at[i], (leader + i, s)
            ).wait_recv()

    product = all_p[0]
    for i in range(1, GROUP):
        product = all_p[i] * product
    group_p[...] = product
    to_later(lambda i: q_copy(i).start())
    back_first.wait_recv()
    back_second.wait_recv()

    def local_errors(lower):
        def plane(z, carry):
            at = pl.ds(pl.multiple_of(z * nx, nx), nx)
            own_at = pl.ds(pl.multiple_of(nx + s * half + z * nx, nx), nx)
            own = [second[own_at], first[own_at]]
            got = [ends[0, at], ends[1, at]]
            finals = own + got if lower else got + own
            error = jnp.zeros((nx, lanes), jnp.float32)
            for k in range(4):
                c = c_own[k, at]
                error = g_own[k, at] * error + (finals[k] - c)
                base[k, at] = error
            block_e[at] = error
            return carry

        lax.fori_loop(0, planes, plane, 0)

    @pl.when(s == 0)
    def _():
        local_errors(True)

    @pl.when(s == 1)
    def _():
        local_errors(False)

    for d in range(1, GROUP):
        e_copy(d).start()
    all_e[member] = block_e[share(member)]
    for i in range(GROUP):
        @pl.when(i != member)
        def _():
            remote(
                block_e.at[share(i)], all_e.at[i], e_send.at[0], e_recv.at[i], (leader + i, s)
            ).wait_recv()

    total = all_e[0]
    for i in range(1, GROUP):
        total = all_p[i] * total + all_e[i]
    group_e[...] = total
    to_later(lambda i: up_copy(i).start())
    leave[0] = jnp.zeros((part, lanes), jnp.float32)
    for i in range(groups - 1):
        @pl.when(i < group)
        def _():
            remote(
                group_p, below_p.at[i], q_send.at[0], q_recv.at[i], (i * GROUP + member, s)
            ).wait_recv()
            remote(
                group_e, below_e.at[i], up_send.at[0], up_recv.at[i], (i * GROUP + member, s)
            ).wait_recv()
            leave[0] = below_p[i] * leave[0] + below_e[i]

    for i in range(GROUP):
        if i:
            leave[i] = all_p[i - 1] * leave[i - 1] + all_e[i - 1]

        @pl.when(i != member)
        def _():
            x_copy(i).start()

    enter[share(member)] = leave[member]

    def finish(d, carry):
        q = lax.rem(member + d, GROUP)

        @pl.when(d > 0)
        def _():
            remote(
                leave.at[q], enter.at[share(q)], x_send.at[q], x_recv.at[q], (leader + q, s)
            ).wait_recv()

        at = share(q)
        entering = enter[at]
        for k in range(4):
            out_ref[k, at] = base[k, at] + cum[k, at] * entering
        return carry

    lax.fori_loop(0, GROUP, finish, 0)

    swap_first.wait_send()
    swap_diff.wait_send()
    swap_vel.wait_send()

    @pl.when(t < n - 1)
    def _():
        to_next.wait_send()

    @pl.when(s == 0)
    def _():
        to_upper.wait_send()

    @pl.when((s == 1) & (t == 0))
    def _():
        to_lower.wait_send()

    back_first.wait_send()
    back_second.wait_send()

    for d in range(1, GROUP):
        p_copy(d).wait_send()
        e_copy(d).wait_send()
        x_copy(lax.rem(member + d, GROUP)).wait_send()

    to_later(lambda i: q_copy(i).wait_send())
    to_later(lambda i: up_copy(i).wait_send())


def fused(c_values, initial, diffusivity, velocity, gains):
    n = lax.axis_size("tm")
    count, nz, nx, ny = c_values.shape
    half = nz * nx
    part = half // GROUP
    f32 = jnp.float32
    dma = pltpu.SemaphoreType.DMA
    field = pltpu.VMEM((2 * half + 2 * nx, ny), f32)
    block = pltpu.VMEM((half, ny), f32)
    four = pltpu.VMEM((4, half, ny), f32)
    shares = pltpu.VMEM((GROUP, part, ny), f32)
    share = pltpu.VMEM((part, ny), f32)
    groups = n // GROUP
    belows = pltpu.VMEM((groups, part, ny), f32)
    error = pl.pallas_call(
        functools.partial(fused_kernel, n, nx, half),
        out_shape=jax.ShapeDtypeStruct((count, half, ny), f32),
        in_specs=[pl.BlockSpec(memory_space=pltpu.HBM)] * 5,
        out_specs=pl.BlockSpec(memory_space=pltpu.VMEM),
        scratch_shapes=[
            four, four,
            pltpu.VMEM((4, 2 * half, ny), f32),
            pltpu.VMEM((7, 2 * half, ny), f32),
            field, field, field,
            pltpu.VMEM((2, half, ny), f32),
            four, four, block, shares, shares, shares, block, belows, belows, share, share,
            dma((7,)), dma((3,)), dma((3,)), dma((3,)), dma((2,)), dma((2,)), dma((2,)),
            dma((GROUP,)), dma((GROUP,)), dma((GROUP,)), dma((GROUP,)), dma((GROUP,)), dma((GROUP,)),
            dma((groups,)), dma((groups,)), dma((groups,)), dma((groups,)),
        ],
        compiler_params=pltpu.CompilerParams(
            collective_id=0, has_side_effects=True, vmem_limit_bytes=32 * 1024 * 1024
        ),
    )(
        pltpu.with_memory_space_constraint(c_values.reshape(count, half, ny), pltpu.HBM),
        pltpu.with_memory_space_constraint(initial.reshape(half, ny), pltpu.HBM),
        pltpu.with_memory_space_constraint(diffusivity.reshape(half, ny), pltpu.HBM),
        pltpu.with_memory_space_constraint(velocity.reshape(3, half, ny), pltpu.HBM),
        pltpu.with_memory_space_constraint(gains.reshape(count, half, ny), pltpu.HBM),
    )
    return c_values + error.reshape(c_values.shape)


def planned(c_values, initial, diffusivity, velocity, gains):
    n, slabs = lax.axis_size("tm"), lax.axis_size("slab")
    count, nz, nx, ny = c_values.shape
    fits = slabs == 2 and count == 4 and n % GROUP == 0 and nx % 8 == 0 and ny % 128 == 0
    if fits and (nz * nx) % (8 * GROUP) == 0:
        return fused(c_values, initial, diffusivity, velocity, gains)
    return body(c_values, initial, diffusivity, velocity, gains)


def solution(mesh):
    placed = (
        P("tm", "slab", None, None),
        P("slab", None, None),
        P("slab", None, None),
        P(None, "slab", None, None),
        P("tm", "slab", None, None),
    )
    return jax.shard_map(
        planned, mesh=mesh, in_specs=placed, out_specs=P("tm", "slab", None, None), check_vma=False
    )
```
